32 devices in a mesh: dp: 16 (over z, y, core), mp: 2 (over x).
Axes of the slice: x: 2, y: 2, z: 4, core: 2. Of those that a mesh axis runs over, the one named last changes fastest.
Arguments:
- image_feat: bfloat16 [2048, 1024], P('dp', 'mp'), may hold values from -6 to 6
- image_proj: bfloat16 [1024, 768], P('mp'), may hold values from -1 to 1
- text_feat: bfloat16 [2048, 768], P('dp', 'mp'), may hold values from -6 to 6
- text_proj: bfloat16 [768, 768], P('mp'), may hold values from -1 to 1
- pair_index: int32 [2048], P('dp'), may hold values from 0 to 2047, each once
- logit_scale: float32 [1], replicated, may hold values from 10 to 100
Outputs:
- row_loss: float32 [2048], P('dp')
- col_loss: float32 [2048], P(('dp', 'mp'))
The draws below stay inside these ranges and needn't reach their ends.
Inputs may be any that keep to these rules, and one draw needn't show every extreme that they name: `pair_index`: each text index appears exactly once.
All inputs are finite; a program needn't handle non-finite values.
Results may differ from the reference program's by a relative error of at most 0.00091.
Values may be sent and summed in bfloat16 or wider, within the bound.
No kernel may reach another device: no remote copies, remote signals or barrier semaphores. Data moves between devices by JAX's collectives and lax.ppermute only.
A program may use at most 64 MiB of HBM per device.

```python
import jax
import jax.numpy as jnp
from jax import lax

WIDTH = 1024
TEXT_WIDTH = 768
EMB = 768
TOKENS = 2048


feature_bound = 6.0


weight_bound = 1.0


def image_weights(key):
    values = jax.random.normal(jax.random.fold_in(key, 11), (WIDTH, EMB), jnp.float32) * WIDTH ** (-0.5)
    return jnp.clip(values, -weight_bound, weight_bound)


def text_weights(key):
    values = jax.random.normal(jax.random.fold_in(key, 12), (TEXT_WIDTH, EMB), jnp.float32) * TEXT_WIDTH ** (-0.5)
    return jnp.clip(values, -weight_bound, weight_bound)


def text_inputs(key):
    features = jnp.clip(jax.random.normal(jax.random.fold_in(key, 13), (TOKENS, TEXT_WIDTH), jnp.float32), -feature_bound, feature_bound)
    return features


def draw_image_proj(key, part):
    return image_weights(key).astype(jnp.bfloat16)


def draw_text_proj(key, part):
    return text_weights(key).astype(jnp.bfloat16)


def draw_text_feat(key, part):
    return text_inputs(key).astype(jnp.bfloat16)


def draw_image_feat(key, part):
    features = jnp.clip(jax.random.normal(jax.random.fold_in(key, 16), (TOKENS, WIDTH), jnp.float32), -feature_bound, feature_bound)
    return features.astype(jnp.bfloat16)


def draw_logit_scale(key, part):
    value = jnp.exp(jax.random.uniform(jax.random.fold_in(key, 17), (1,), jnp.float32, jnp.log(10.0), jnp.log(100.0)))
    return jnp.clip(value, 10.0, 100.0)


def setup_inputs(seed: int = 0) -> dict:
    splits = jax.random.split(jax.random.key(seed), 7)
    return {
        "image_feat": draw_image_feat(jax.random.fold_in(splits[6], 71), 0),
        "image_proj": draw_image_proj(jax.random.fold_in(splits[6], 71), 0),
        "text_feat": draw_text_feat(jax.random.fold_in(splits[6], 71), 0),
        "text_proj": draw_text_proj(jax.random.fold_in(splits[6], 71), 0),
        "pair_index": jax.random.permutation(splits[4], TOKENS).astype(jnp.int32),
        "logit_scale": draw_logit_scale(jax.random.fold_in(splits[6], 71), 0),
    }


def embed(features, projection):
    raw = jnp.dot(features.astype(jnp.float32), projection.astype(jnp.float32), preferred_element_type=jnp.float32)
    norm_sq = lax.optimization_barrier(jnp.sum(raw * raw, axis=1, keepdims=True))
    return (raw / jnp.sqrt(norm_sq + 1e-06)).astype(jnp.bfloat16)

def reference(image_feat, image_proj, text_feat, text_proj, pair_index, logit_scale):
    image_emb = embed(image_feat, image_proj)
    text_emb = embed(text_feat, text_proj)
    multiplier = logit_scale[0]
    block_rows = min(1024, TOKENS)
    block_count = TOKENS // block_rows

    def row_block(index):
        rows = lax.dynamic_slice_in_dim(image_emb, index * block_rows, block_rows, 0)
        logits = multiplier * lax.dot_general(rows.astype(jnp.float32), text_emb.astype(jnp.float32), (((1,), (1,)), ((), ())), preferred_element_type=jnp.float32)
        return jax.nn.logsumexp(logits, axis=1)

    def col_block(index):
        cols = lax.dynamic_slice_in_dim(text_emb, index * block_rows, block_rows, 0)
        logits = multiplier * lax.dot_general(cols.astype(jnp.float32), image_emb.astype(jnp.float32), (((1,), (1,)), ((), ())), preferred_element_type=jnp.float32)
        return jax.nn.logsumexp(logits, axis=1)
    indices = jnp.arange(block_count, dtype=jnp.int32)
    row_lse = lax.map(row_block, indices).reshape(TOKENS)
    col_lse = lax.map(col_block, indices).reshape(TOKENS)
    paired = text_emb[pair_index].astype(jnp.float32)
    positive = multiplier * lax.optimization_barrier(jnp.sum(image_emb.astype(jnp.float32) * paired, axis=1))
    col_positive = jnp.zeros((TOKENS,), jnp.float32).at[pair_index].set(positive)
    return (row_lse - positive, col_lse - col_positive)
```

```python
import jax
import jax.numpy as jnp
from jax import lax
from jax.sharding import PartitionSpec as P


def exchange(value, axis, count, stride):
    return lax.ppermute(value, axis, [(i, i ^ stride) for i in range(count)])


def normalize(raw):
    norm_sq = jnp.sum(raw * raw, axis=1, keepdims=True)
    return (raw / jnp.sqrt(norm_sq + 1e-06)).astype(jnp.bfloat16)


def merge(own, other):
    top = jnp.maximum(own[0], other[0])
    total = jnp.exp(own[0] - top) + jnp.exp(other[0] - top)
    return jnp.stack([top + jnp.log(total), own[1] + other[1]])


def strides(low, high):
    out = []
    while low < high:
        out.append(low)
        low *= 2
    return out


def on_device(image_feat, image_proj, text_feat, text_proj, pair_index, logit_scale):
    dp = lax.axis_size("dp")
    mp = lax.axis_size("mp")
    dp_index = lax.axis_index("dp")
    mp_index = lax.axis_index("mp")
    levels = dp.bit_length() - 1
    far = 1 << (levels // 2)
    near = dp // far
    core = min(2, near)
    rows = image_feat.shape[0]
    half = rows // mp

    def text_rows(owner):
        mine = lax.dynamic_slice_in_dim(text_feat, owner * half, half, 0)
        return jnp.dot(mine, text_proj, preferred_element_type=jnp.float32)

    text_raw = None
    got = [
        exchange(text_rows(mp_index ^ step).astype(jnp.float16), "mp", mp, step)
        for step in range(1, mp)
    ]
    text_raw = text_rows(mp_index)
    image_raw = jnp.dot(image_feat, image_proj, preferred_element_type=jnp.float32)
    for step in strides(1, mp):
        image_raw = image_raw + exchange(image_raw.astype(jnp.float16), "mp", mp, step)
    for part in got:
        text_raw = text_raw + part

    pairs = pair_index[None]
    for stride in strides(core, near):
        pairs = jnp.concatenate([pairs, exchange(pairs, "dp", dp, stride)])

    text_emb = normalize(text_raw)
    texts = [text_emb] + [exchange(text_emb, "dp", dp, near * j) for j in range(1, far)]
    image_emb = normalize(image_raw)[None]
    for stride in strides(core, near):
        image_emb = jnp.concatenate([image_emb, exchange(image_emb, "dp", dp, stride)])
    both = [[text] + [exchange(text, "dp", dp, c) for c in range(1, core)] for text in texts]
    text_all = jnp.concatenate([text for c in range(core) for text in [b[c] for b in both]])

    images = image_emb.reshape(-1, image_emb.shape[-1])
    logits = logit_scale[0] * lax.dot_general(
        images, text_all, (((1,), (1,)), ((), ())), preferred_element_type=jnp.float32
    )
    slot = jnp.arange(core * far, dtype=jnp.int32)
    owner = dp_index ^ (near * (slot % far) + slot // far)
    start = owner * rows + mp_index * half
    text_id = (start[:, None] + jnp.arange(half, dtype=jnp.int32)[None]).reshape(-1)
    picked = jnp.where(pairs.reshape(-1, 1) == text_id[None], logits, 0.0)

    row_top = jnp.max(logits, axis=1)
    row_lse = row_top + jnp.log(jnp.sum(jnp.exp(logits - row_top[:, None]), axis=1))
    col_top = jnp.max(logits, axis=0)
    col_lse = col_top + jnp.log(jnp.sum(jnp.exp(logits - col_top[None]), axis=0))
    row = jnp.stack([row_lse, jnp.sum(picked, axis=1)])
    col = jnp.stack([col_lse, jnp.sum(picked, axis=0)])

    for stride in [1] * (core > 1) + [near * s for s in reversed(strides(1, far))]:
        split = col.shape[1] // 2
        col = merge(col[:, :split], exchange(col[:, split:], "dp", dp, stride))
    for stride in reversed(strides(core, near)):
        split = row.shape[1] // 2
        row = merge(row[:, :split], exchange(row[:, split:], "dp", dp, stride))
    for step in strides(1, mp):
        row = merge(row, exchange(row, "mp", mp, step))
    return (row[0] - row[1], col[0] - col[1])


def solution(mesh):
    in_specs = (P("dp", "mp"), P("mp", None), P("dp", "mp"), P("mp", None), P("dp"), P())
    out_specs = (P("dp"), P(("dp", "mp")))
    return jax.shard_map(
        on_device, mesh=mesh, in_specs=in_specs, out_specs=out_specs, check_vma=False
    )
```

```python
import functools

import jax
import jax.numpy as jnp
from jax import lax
from jax.experimental import pallas as pl
from jax.experimental.pallas import tpu as pltpu
from jax.sharding import PartitionSpec as P


def exchange(value, stride, step=0):
    dp, mp = lax.axis_size("dp"), lax.axis_size("mp")
    pairs = [(i * mp + j, (i ^ stride) * mp + (j ^ step)) for i in range(dp) for j in range(mp)]
    return lax.ppermute(value, ("dp", "mp"), pairs)


def normalize(raw):
    norm_sq = jnp.sum(raw * raw, axis=1, keepdims=True)
    return (raw / jnp.sqrt(norm_sq + 1e-06)).astype(jnp.bfloat16)


def join(stats):
    top = functools.reduce(jnp.maximum, [s[0] for s in stats])
    total = sum(jnp.exp(s[0] - top) for s in stats)
    return jnp.stack([top + jnp.log(total), sum(s[1] for s in stats)])


def stats_kernel(n_image, n_text, scale_ref, start_ref, *refs):
    refs = list(refs)
    images = [refs.pop(0) for _ in range(n_image)]
    pairs = [refs.pop(0) for _ in range(n_image)]
    texts = [refs.pop(0) for _ in range(n_text)]
    col_out = [refs.pop(0) for _ in range(len(refs) - n_image)]
    row_out = refs
    rows = images[0].shape[0]
    half = texts[0].shape[0]
    per_out = n_text // len(col_out)
    image = jnp.concatenate([r[...] for r in images], axis=0)
    text = jnp.concatenate([r[...] for r in texts], axis=0)
    logits = scale_ref[0] * lax.dot_general(
        image, text, (((1,), (1,)), ((), ())), preferred_element_type=jnp.float32
    )
    place = lax.broadcasted_iota(jnp.int32, (1, n_text * half), 1)
    ids = place + start_ref[0]
    for k in range(1, n_text):
        ids = jnp.where(place >= k * half, place + (start_ref[k] - k * half), ids)
    pair = jnp.concatenate([jnp.broadcast_to(r[...], (rows, rows)).T for r in pairs], axis=0)
    pair = jnp.concatenate([pair] * (n_text * half // rows), axis=1)
    picked = jnp.where(pair == ids, logits, 0.0)

    top = jnp.max(logits, axis=0, keepdims=True)
    lse = top + jnp.log(jnp.sum(jnp.exp(logits - top), axis=0, keepdims=True))
    positive = jnp.sum(picked, axis=0, keepdims=True)
    for k, out in enumerate(col_out):
        lanes = slice(k * per_out * half, (k + 1) * per_out * half)
        out[0:1, :] = lse[:, lanes]
        out[1:2, :] = positive[:, lanes]

    top = jnp.max(logits, axis=1, keepdims=True)
    lse = top + jnp.log(jnp.sum(jnp.exp(logits - top), axis=1, keepdims=True))
    positive = jnp.sum(picked, axis=1, keepdims=True)
    for k, out in enumerate(row_out):
        block = slice(k * rows, (k + 1) * rows)
        lane = lax.broadcasted_iota(jnp.int32, (rows, rows), 1)
        both = jnp.where(lane == 0, lse[block], positive[block]).T
        out[...] = both[0:2]


def block_stats(scale, starts, images, pairs, texts, n_out):
    rows = images[0].shape[0]
    count = len(texts) * texts[0].shape[0]
    vmem = pl.BlockSpec(memory_space=pltpu.VMEM)
    smem = pl.BlockSpec(memory_space=pltpu.SMEM)
    operands = [*images, *pairs, *texts]
    out = pl.pallas_call(
        functools.partial(stats_kernel, len(images), len(texts)),
        out_shape=[jax.ShapeDtypeStruct((2, count // n_out), jnp.float32)] * n_out
        + [jax.ShapeDtypeStruct((2, rows), jnp.float32)] * len(images),
        in_specs=[smem, smem] + [vmem] * len(operands),
        out_specs=[vmem] * (n_out + len(images)),
        compiler_params=pltpu.CompilerParams(vmem_limit_bytes=48 * 2**20),
        cost_estimate=pl.CostEstimate(
            flops=2 * rows * len(images) * count * images[0].shape[1],
            bytes_accessed=sum(o.size * o.dtype.itemsize for o in operands),
            transcendentals=2 * rows * len(images) * count,
        ),
    )(scale, starts, *operands)
    return out[:n_out], out[n_out:]


def on_device(image_feat, image_proj, text_feat, text_proj, pair_index, logit_scale):
    dp = lax.axis_size("dp")
    mp = lax.axis_size("mp")
    dp_index = lax.axis_index("dp")
    mp_index = lax.axis_index("mp")
    far = 1 << ((dp.bit_length() - 1) // 2)
    near = dp // far
    core = min(2, near)
    rows = image_feat.shape[0]
    half = rows // mp
    width = text_proj.shape[1]
    z_order = list(reversed(range(1, far)))

    def text_rows(owner):
        mine = lax.dynamic_slice_in_dim(text_feat, owner * half, half, 0)
        return jnp.dot(mine, text_proj, preferred_element_type=jnp.float32)

    got = [
        exchange(text_rows(mp_index ^ step).astype(jnp.float16), 0, step)
        for step in range(1, mp)
    ]
    image_raw = jnp.dot(image_feat, image_proj, preferred_element_type=jnp.float32)
    sent = image_raw.astype(jnp.float16)
    for step in range(1, mp):
        image_raw = image_raw + exchange(sent, 0, step)
    text_emb = normalize(sum(got, text_rows(mp_index)))

    texts = {j: exchange(text_emb, near * j) for j in z_order}

    pairs = [pair_index[None]]
    pairs += [exchange(pairs[0], stride) for stride in range(core, near, core)]
    image_emb, *pairs = lax.optimization_barrier((normalize(image_raw), *pairs))
    images = [image_emb] + [exchange(image_emb, stride) for stride in range(core, near, core)]

    texts[0] = text_emb
    late, _ = lax.optimization_barrier((text_emb, texts[z_order[0]]))
    both = [
        text for j in range(far)
        for text in [texts[j]] + [exchange(late if j == 0 else texts[j], c) for c in range(1, core)]
    ]
    owner = jnp.stack([dp_index ^ (near * j + c) for j in range(far) for c in range(core)])
    starts = (owner * rows + mp_index * half).astype(jnp.int32)
    col, row = block_stats(logit_scale, starts, images, pairs, both, far)

    k = far
    col = list(col)
    while k > 1:
        k //= 2
        other = exchange(jnp.concatenate(col[k : 2 * k], axis=1), near * k)
        n = core * half
        col = [join([col[j], other[:, j * n : (j + 1) * n]]) for j in range(k)]
    col = col[0]
    row = list(row)
    k = near // core
    while k > 1:
        k //= 2
        row = [join([row[s], exchange(row[s + k], core * k)]) for s in range(k)]
    row = join([row[0]] + [exchange(row[0], 0, m) for m in range(1, mp)])
    col = join(
        [col[:, :half]]
        + [exchange(col[:, c * half : (c + 1) * half], c) for c in range(1, core)]
    )
    return (row[0] - row[1], col[0] - col[1])


def solution(mesh):
    in_specs = (P("dp", "mp"), P("mp", None), P("dp", "mp"), P("mp", None), P("dp"), P())
    out_specs = (P("dp"), P(("dp", "mp")))
    return jax.shard_map(
        on_device, mesh=mesh, in_specs=in_specs, out_specs=out_specs, check_vma=False
    )
```

```python
import functools

import jax
import jax.numpy as jnp
from jax import lax
from jax.experimental import pallas as pl
from jax.experimental.pallas import tpu as pltpu
from jax.sharding import PartitionSpec as P


def exchange(value, stride, step=0):
    dp, mp = lax.axis_size("dp"), lax.axis_size("mp")
    pairs = [(i * mp + j, (i ^ stride) * mp + (j ^ step)) for i in range(dp) for j in range(mp)]
    return lax.ppermute(value, ("dp", "mp"), pairs)


def normalize(raw):
    norm_sq = jnp.sum(raw * raw, axis=1, keepdims=True)
    return (raw / jnp.sqrt(norm_sq + 1e-06)).astype(jnp.bfloat16)


def join(stats):
    top = functools.reduce(jnp.maximum, [s[0] for s in stats])
    total = sum(jnp.exp(s[0] - top) for s in stats)
    return jnp.stack([top + jnp.log(total), sum(s[1] for s in stats)])


def stats_kernel(n_image, n_text, scale_ref, id_ref, *refs):
    refs = list(refs)
    texts = [refs.pop(0)]
    images = [refs.pop(0) for _ in range(n_image)]
    pairs = [refs.pop(0) for _ in range(n_image)]
    texts += [refs.pop(0) for _ in range(n_text - 1)]
    col_out = [refs.pop(0) for _ in range(len(refs) - n_image)]
    row_out = refs
    rows = images[0].shape[0]
    half = texts[0].shape[0]
    per_out = n_text // len(col_out)
    image = jnp.concatenate([r[...] for r in images], axis=0)
    text = jnp.concatenate([r[...] for r in texts], axis=0)
    logits = scale_ref[0:1, 0:1] * lax.dot_general(
        image, text, (((1,), (1,)), ((), ())), preferred_element_type=jnp.float32
    )
    ids = id_ref[...]
    pair = jnp.concatenate([jnp.broadcast_to(r[...], (rows, rows)).T for r in pairs], axis=0)
    pair = jnp.concatenate([pair] * (n_text * half // rows), axis=1)
    picked = jnp.where(pair == ids, logits, 0.0)

    top = jnp.max(logits, axis=0, keepdims=True)
    lse = top + jnp.log(jnp.sum(jnp.exp(logits - top), axis=0, keepdims=True))
    positive = jnp.sum(picked, axis=0, keepdims=True)
    for k, out in enumerate(col_out):
        lanes = slice(k * per_out * half, (k + 1) * per_out * half)
        out[0:1, :] = lse[:, lanes]
        out[1:2, :] = positive[:, lanes]

    top = jnp.max(logits, axis=1, keepdims=True)
    lse = top + jnp.log(jnp.sum(jnp.exp(logits - top), axis=1, keepdims=True))
    positive = jnp.sum(picked, axis=1, keepdims=True)
    for k, out in enumerate(row_out):
        block = slice(k * rows, (k + 1) * rows)
        lane = lax.broadcasted_iota(jnp.int32, (rows, rows), 1)
        both = jnp.where(lane == 0, lse[block], positive[block]).T
        out[...] = both[0:2]


def block_stats(scale, ids, images, pairs, texts, n_out):
    rows = images[0].shape[0]
    count = len(texts) * texts[0].shape[0]
    vmem = pl.BlockSpec(memory_space=pltpu.VMEM)
    operands = [scale, ids, texts[0], *images, *pairs, *texts[1:]]
    out = pl.pallas_call(
        functools.partial(stats_kernel, len(images), len(texts)),
        out_shape=[jax.ShapeDtypeStruct((2, count // n_out), jnp.float32)] * n_out
        + [jax.ShapeDtypeStruct((2, rows), jnp.float32)] * len(images),
        in_specs=[vmem] * len(operands),
        out_specs=[vmem] * (n_out + len(images)),
        compiler_params=pltpu.CompilerParams(vmem_limit_bytes=48 * 2**20),
        cost_estimate=pl.CostEstimate(
            flops=2 * rows * len(images) * count * images[0].shape[1],
            bytes_accessed=sum(o.size * o.dtype.itemsize for o in operands),
            transcendentals=2 * rows * len(images) * count,
        ),
    )(*operands)
    return out[:n_out], out[n_out:]


def on_device(image_feat, image_proj, text_feat, text_proj, pair_index, logit_scale):
    dp = lax.axis_size("dp")
    mp = lax.axis_size("mp")
    dp_index = lax.axis_index("dp")
    mp_index = lax.axis_index("mp")
    far = 1 << ((dp.bit_length() - 1) // 2)
    near = dp // far
    core = min(2, near)
    rows = image_feat.shape[0]
    half = rows // mp
    width = text_proj.shape[1]
    z_order = list(reversed(range(1, far)))

    def text_rows(owner):
        mine = lax.dynamic_slice_in_dim(text_feat, owner * half, half, 0)
        return jnp.dot(mine, text_proj, preferred_element_type=jnp.float32)

    got = [
        exchange(text_rows(mp_index ^ step).astype(jnp.float16), 0, step)
        for step in range(1, mp)
    ]
    image_raw = jnp.dot(image_feat, image_proj, preferred_element_type=jnp.float32)
    sent = image_raw.astype(jnp.float16)
    for step in range(1, mp):
        image_raw = image_raw + exchange(sent, 0, step)
    text_emb = normalize(sum(got, lax.optimization_barrier(text_rows(mp_index))))

    texts = {j: exchange(text_emb, near * j) for j in z_order}

    pairs = [pair_index[None]]
    pairs += [exchange(pairs[0], stride) for stride in range(core, near, core)]
    image_emb, *pairs = lax.optimization_barrier((normalize(image_raw), *pairs))
    images = [image_emb] + [exchange(image_emb, stride) for stride in range(core, near, core)]

    texts[0] = text_emb
    late, _ = lax.optimization_barrier((text_emb, texts[z_order[1]]))
    both = [
        text for j in range(far)
        for text in [texts[j]] + [exchange(late if j == 0 else texts[j], c) for c in range(1, core)]
    ]
    owner = jnp.stack([dp_index ^ (near * j + c) for j in range(far) for c in range(core)])
    starts = (owner * rows + mp_index * half).astype(jnp.int32)
    ids = (starts[:, None] + jnp.arange(half, dtype=jnp.int32)[None]).reshape(1, -1)
    scale = jnp.broadcast_to(logit_scale[None], (1, rows))
    col, row = block_stats(scale, ids, images, pairs, both, far)

    k = far
    col = list(col)
    while k > 1:
        k //= 2
        other = exchange(jnp.concatenate(col[k : 2 * k], axis=1), near * k)
        n = core * half
        col = [join([col[j], other[:, j * n : (j + 1) * n]]) for j in range(k)]
    col = col[0]
    row = list(row)
    k = near // core
    while k > 1:
        k //= 2
        row = [join([row[s], exchange(row[s + k], core * k)]) for s in range(k)]
    row = join([row[0]] + [exchange(row[0], 0, m) for m in range(1, mp)])
    col = join(
        [col[:, :half]]
        + [exchange(col[:, c * half : (c + 1) * half], c) for c in range(1, core)]
    )
    return (row[0] - row[1], col[0] - col[1])


def solution(mesh):
    in_specs = (P("dp", "mp"), P("mp", None), P("dp", "mp"), P("mp", None), P("dp"), P())
    out_specs = (P("dp"), P(("dp", "mp")))
    return jax.shard_map(
        on_device, mesh=mesh, in_specs=in_specs, out_specs=out_specs, check_vma=False
    )
```

```python
import functools

import jax
import jax.numpy as jnp
from jax import lax
from jax.experimental import pallas as pl
from jax.experimental.pallas import tpu as pltpu
from jax.sharding import PartitionSpec as P


def exchange(value, stride, step=0):
    dp, mp = lax.axis_size("dp"), lax.axis_size("mp")
    pairs = [(i * mp + j, (i ^ stride) * mp + (j ^ step)) for i in range(dp) for j in range(mp)]
    return lax.ppermute(value, ("dp", "mp"), pairs)


def normalize(raw):
    norm_sq = jnp.sum(raw * raw, axis=1, keepdims=True)
    return (raw / jnp.sqrt(norm_sq + 1e-06)).astype(jnp.bfloat16)


def join(stats):
    top = functools.reduce(jnp.maximum, [s[0] for s in stats])
    total = sum(jnp.exp(s[0] - top) for s in stats)
    return jnp.stack([top + jnp.log(total), sum(s[1] for s in stats)])


def stats_kernel(n_image, places, n_col, scale_ref, id_ref, *refs):
    refs = list(refs)
    texts = [refs.pop(0)]
    images = [refs.pop(0) for _ in range(n_image)]
    pairs = [refs.pop(0) for _ in range(n_image)]
    texts += [refs.pop(0) for _ in places[1:]]
    texts = [text for _, text in sorted(zip(places, texts), key=lambda pair: pair[0])]
    col_out, row_out = refs[:n_col], refs[n_col:]
    rows = images[0].shape[0]
    half = texts[0].shape[0]
    image = jnp.concatenate([r[...] for r in images], axis=0)
    text = jnp.concatenate([r[...] for r in texts], axis=0)
    logits = scale_ref[0:1, 0:1] * lax.dot_general(
        image, text, (((1,), (1,)), ((), ())), preferred_element_type=jnp.float32
    )
    ids = id_ref[...]
    pair = jnp.concatenate([jnp.broadcast_to(r[...], (rows, rows)).T for r in pairs], axis=0)
    pair = jnp.concatenate([pair] * (len(texts) * half // rows), axis=1)
    picked = jnp.where(pair == ids, logits, 0.0)

    top = jnp.max(logits, axis=0, keepdims=True)
    lse = top + jnp.log(jnp.sum(jnp.exp(logits - top), axis=0, keepdims=True))
    positive = jnp.sum(picked, axis=0, keepdims=True)
    write(col_out, lse, positive)

    top = jnp.max(logits, axis=1, keepdims=True)
    lse = top + jnp.log(jnp.sum(jnp.exp(logits - top), axis=1, keepdims=True))
    positive = jnp.sum(picked, axis=1, keepdims=True)
    lane = lax.broadcasted_iota(jnp.int32, (image.shape[0], rows), 1)
    both = jnp.where(lane == 0, lse, positive).T
    write(row_out, both[0:1], both[1:2])


def write(outs, lse, positive):
    count = lse.shape[1] // len(outs)
    for k, out in enumerate(outs):
        out[0:1, :] = lse[:, k * count : (k + 1) * count]
        out[1:2, :] = positive[:, k * count : (k + 1) * count]


def pieces(count, n):
    return [jax.ShapeDtypeStruct((2, count // n), jnp.float32)] * n


def block_stats(scale, ids, images, pairs, texts, places):
    rows = images[0].shape[0]
    count = len(texts) * texts[0].shape[0]
    vmem = pl.BlockSpec(memory_space=pltpu.VMEM)
    operands = [scale, ids, texts[0], *images, *pairs, *texts[1:]]
    col = pieces(count, min(2, len(texts)))
    row = pieces(rows * len(images), min(2, len(images)))
    out = pl.pallas_call(
        functools.partial(stats_kernel, len(images), places, len(col)),
        out_shape=col + row,
        in_specs=[vmem] * len(operands),
        out_specs=[vmem] * len(col + row),
        compiler_params=pltpu.CompilerParams(vmem_limit_bytes=48 * 2**20),
        cost_estimate=pl.CostEstimate(
            flops=2 * rows * len(images) * count * images[0].shape[1],
            bytes_accessed=sum(o.size * o.dtype.itemsize for o in operands),
            transcendentals=2 * rows * len(images) * count,
        ),
    )(*operands)
    return out[: len(col)], out[len(col) :]


def joined(parts):
    top = functools.reduce(jnp.maximum, [p[0:1, :] for p in parts])
    total = sum(jnp.exp(p[0:1, :] - top) for p in parts)
    return top + jnp.log(total), sum(p[1:2, :] for p in parts)


def join_kernel(counts, splits, *refs):
    refs = list(refs)
    groups = [[refs.pop(0) for _ in range(n)] for n in counts]
    for parts, n in zip(groups, splits):
        lse, positive = joined(parts)
        if n:
            write([refs.pop(0) for _ in range(n)], lse, positive)
        else:
            refs.pop(0)[...] = lse - positive


def join(groups, splits):
    vmem = pl.BlockSpec(memory_space=pltpu.VMEM)
    parts = [part for group in groups for part in group]
    shapes = [
        pieces(g[0].shape[1], n) if n else [jax.ShapeDtypeStruct((1, g[0].shape[1]), jnp.float32)]
        for g, n in zip(groups, splits)
    ]
    flat = [s for shape in shapes for s in shape]
    out = list(pl.pallas_call(
        functools.partial(join_kernel, [len(g) for g in groups], splits),
        out_shape=flat,
        in_specs=[vmem] * len(parts),
        out_specs=[vmem] * len(flat),
        compiler_params=pltpu.CompilerParams(vmem_limit_bytes=4 * 2**20),
    )(*parts))
    return [[out.pop(0) for _ in shape] for shape in shapes]


def on_device(image_feat, image_proj, text_feat, text_proj, pair_index, logit_scale):
    dp = lax.axis_size("dp")
    mp = lax.axis_size("mp")
    dp_index = lax.axis_index("dp")
    mp_index = lax.axis_index("mp")
    far = 1 << ((dp.bit_length() - 1) // 2)
    near = dp // far
    core = min(2, near)
    rows = image_feat.shape[0]
    half = rows // mp
    width = text_proj.shape[1]
    z_order = list(reversed(range(1, far)))

    def text_rows(owner):
        mine = lax.dynamic_slice_in_dim(text_feat, owner * half, half, 0)
        return jnp.dot(mine, text_proj, preferred_element_type=jnp.float32)

    got = [
        exchange(text_rows(mp_index ^ step).astype(jnp.float16), 0, step)
        for step in range(1, mp)
    ]
    image_raw = jnp.dot(image_feat, image_proj, preferred_element_type=jnp.float32)
    sent = image_raw.astype(jnp.float16)
    for step in range(1, mp):
        image_raw = image_raw + exchange(sent, 0, step)
    text_emb = normalize(sum(got, lax.optimization_barrier(text_rows(mp_index))))

    texts = {j: exchange(text_emb, near * j) for j in z_order}

    pairs = [pair_index[None]]
    pairs += [exchange(pairs[0], stride) for stride in range(core, near, core)]
    image_emb, *pairs = lax.optimization_barrier((normalize(image_raw), *pairs))
    images = [image_emb] + [exchange(image_emb, stride) for stride in range(core, near, core)]

    texts[0] = text_emb
    late, _ = lax.optimization_barrier((text_emb, texts[z_order[1]]))
    blocks = {(0, j): texts[j] for j in range(far)}
    for c in range(1, core):
        blocks.update({(c, j): exchange(texts[j] if j else late, c) for j in range(far)})
    z_names = sorted(z_order, key=lambda j: (j != far // 2, -j))
    order = [(0, 0)] + [(c, j) for j in z_names for c in range(core)] + [(c, 0) for c in range(1, core)]
    owner = jnp.stack([dp_index ^ (near * j + c) for c in range(core) for j in range(far)])
    starts = (owner * rows + mp_index * half).astype(jnp.int32)
    ids = (starts[:, None] + jnp.arange(half, dtype=jnp.int32)[None]).reshape(1, -1)
    scale = jnp.broadcast_to(logit_scale[None], (1, rows))
    col, row = block_stats(
        scale, ids, images, pairs, [blocks[k] for k in order], [c * far + j for c, j in order]
    )

    col_steps = [1] * (core > 1) + [near << k for k in reversed(range(far.bit_length() - 1))]
    row_steps = [core << k for k in reversed(range((near // core).bit_length() - 1))]
    while len(col_steps) > 1:
        ((*col,),) = join([[col[0], exchange(col[1], col_steps.pop(0))]], [2])
    while row_steps:
        ((*row,),) = join([[row[0], exchange(row[1], row_steps.pop(0))]], [2 if row_steps else 1])
    row = [row[0]] + [exchange(row[0], 0, m) for m in range(1, mp)]
    col = [col[0], exchange(col[1], col_steps.pop(0))]
    (col_loss,), (row_loss,) = join([col, row], [0, 0])
    return (row_loss.reshape(-1), col_loss.reshape(-1))


def solution(mesh):
    in_specs = (P("dp", "mp"), P("mp", None), P("dp", "mp"), P("mp", None), P("dp"), P())
    out_specs = (P("dp"), P(("dp", "mp")))
    return jax.shard_map(
        on_device, mesh=mesh, in_specs=in_specs, out_specs=out_specs, check_vma=False
    )
```

```python
import functools

import jax
import jax.numpy as jnp
from jax import lax
from jax.experimental import pallas as pl
from jax.experimental.pallas import tpu as pltpu
from jax.sharding import PartitionSpec as P


def exchange(value, stride, step=0):
    dp, mp = lax.axis_size("dp"), lax.axis_size("mp")
    pairs = [(i * mp + j, (i ^ stride) * mp + (j ^ step)) for i in range(dp) for j in range(mp)]
    return lax.ppermute(value, ("dp", "mp"), pairs)


def normalize(raw):
    norm_sq = jnp.sum(raw * raw, axis=1, keepdims=True)
    return (raw / jnp.sqrt(norm_sq + 1e-06)).astype(jnp.bfloat16)


def join(stats):
    top = functools.reduce(jnp.maximum, [s[0] for s in stats])
    total = sum(jnp.exp(s[0] - top) for s in stats)
    return jnp.stack([top + jnp.log(total), sum(s[1] for s in stats)])


def stats_kernel(n_image, places, n_col, scale_ref, id_ref, *refs):
    refs = list(refs)
    texts = [refs.pop(0)]
    images = [refs.pop(0) for _ in range(n_image)]
    pairs = [refs.pop(0) for _ in range(n_image)]
    texts += [refs.pop(0) for _ in places[1:]]
    half = texts[0].shape[0]
    blocks = {}
    for held, text in zip(places, texts):
        blocks.update({place: text[n * half : (n + 1) * half, :] for n, place in enumerate(held)})
    texts = [blocks[place] for place in sorted(blocks)]
    col_out, row_out = refs[:n_col], refs[n_col:]
    rows = images[0].shape[0]
    image = jnp.concatenate([r[...] for r in images], axis=0)
    text = jnp.concatenate(texts, axis=0)
    logits = scale_ref[0:1, 0:1] * lax.dot_general(
        image, text, (((1,), (1,)), ((), ())), preferred_element_type=jnp.float32
    )
    ids = id_ref[...]
    pair = jnp.concatenate([jnp.broadcast_to(r[...], (rows, rows)).T for r in pairs], axis=0)
    pair = jnp.concatenate([pair] * (len(texts) * half // rows), axis=1)
    picked = jnp.where(pair == ids, logits, 0.0)

    top = jnp.max(logits, axis=0, keepdims=True)
    lse = top + jnp.log(jnp.sum(jnp.exp(logits - top), axis=0, keepdims=True))
    positive = jnp.sum(picked, axis=0, keepdims=True)
    write(col_out, lse, positive)

    top = jnp.max(logits, axis=1, keepdims=True)
    lse = top + jnp.log(jnp.sum(jnp.exp(logits - top), axis=1, keepdims=True))
    positive = jnp.sum(picked, axis=1, keepdims=True)
    lane = lax.broadcasted_iota(jnp.int32, (image.shape[0], rows), 1)
    both = jnp.where(lane == 0, lse, positive).T
    write(row_out, both[0:1], both[1:2])


def write(outs, lse, positive):
    count = lse.shape[1] // len(outs)
    for k, out in enumerate(outs):
        out[0:1, :] = lse[:, k * count : (k + 1) * count]
        out[1:2, :] = positive[:, k * count : (k + 1) * count]


def pieces(count, n):
    return [jax.ShapeDtypeStruct((2, count // n), jnp.float32)] * n


def block_stats(scale, ids, images, pairs, texts, places):
    rows = images[0].shape[0]
    count = sum(text.shape[0] for text in texts)
    vmem = pl.BlockSpec(memory_space=pltpu.VMEM)
    operands = [scale, ids, texts[0], *images, *pairs, *texts[1:]]
    col = pieces(count, 2)
    row = pieces(rows * len(images), min(2, len(images)))
    out = pl.pallas_call(
        functools.partial(stats_kernel, len(images), places, len(col)),
        out_shape=col + row,
        in_specs=[vmem] * len(operands),
        out_specs=[vmem] * len(col + row),
        compiler_params=pltpu.CompilerParams(vmem_limit_bytes=48 * 2**20),
        cost_estimate=pl.CostEstimate(
            flops=2 * rows * len(images) * count * images[0].shape[1],
            bytes_accessed=sum(o.size * o.dtype.itemsize for o in operands),
            transcendentals=2 * rows * len(images) * count,
        ),
    )(*operands)
    return out[: len(col)], out[len(col) :]


def joined(parts):
    top = functools.reduce(jnp.maximum, [p[0:1, :] for p in parts])
    total = sum(jnp.exp(p[0:1, :] - top) for p in parts)
    return top + jnp.log(total), sum(p[1:2, :] for p in parts)


def join_kernel(counts, splits, *refs):
    refs = list(refs)
    groups = [[refs.pop(0) for _ in range(n)] for n in counts]
    for parts, n in zip(groups, splits):
        lse, positive = joined(parts)
        if n:
            write([refs.pop(0) for _ in range(n)], lse, positive)
        else:
            refs.pop(0)[...] = lse - positive


def join(groups, splits):
    vmem = pl.BlockSpec(memory_space=pltpu.VMEM)
    parts = [part for group in groups for part in group]
    shapes = [
        pieces(g[0].shape[1], n) if n else [jax.ShapeDtypeStruct((1, g[0].shape[1]), jnp.float32)]
        for g, n in zip(groups, splits)
    ]
    flat = [s for shape in shapes for s in shape]
    out = list(pl.pallas_call(
        functools.partial(join_kernel, [len(g) for g in groups], splits),
        out_shape=flat,
        in_specs=[vmem] * len(parts),
        out_specs=[vmem] * len(flat),
        compiler_params=pltpu.CompilerParams(vmem_limit_bytes=4 * 2**20),
    )(*parts))
    return [[out.pop(0) for _ in shape] for shape in shapes]


def on_device(image_feat, image_proj, text_feat, text_proj, pair_index, logit_scale):
    dp = lax.axis_size("dp")
    mp = lax.axis_size("mp")
    dp_index = lax.axis_index("dp")
    mp_index = lax.axis_index("mp")
    far = 1 << ((dp.bit_length() - 1) // 2)
    near = dp // far
    core = min(2, near)
    rows = image_feat.shape[0]
    half = rows // mp
    width = text_proj.shape[1]
    z_order = list(reversed(range(1, far)))

    def text_rows(owner):
        mine = lax.dynamic_slice_in_dim(text_feat, owner * half, half, 0)
        return jnp.dot(mine, text_proj, preferred_element_type=jnp.float32)

    got = [
        exchange(text_rows(mp_index ^ step).astype(jnp.float16), 0, step)
        for step in range(1, mp)
    ]
    image_raw = jnp.dot(image_feat, image_proj, preferred_element_type=jnp.float32)
    sent = image_raw.astype(jnp.float16)
    for step in range(1, mp):
        image_raw = image_raw + exchange(sent, 0, step)
    text_emb = normalize(sum(got, lax.optimization_barrier(text_rows(mp_index))))

    texts = {j: exchange(text_emb, near * j) for j in z_order}

    pairs = [pair_index[None]]
    pairs += [exchange(pairs[0], stride) for stride in range(core, near, core)]
    image_emb, *pairs = lax.optimization_barrier((normalize(image_raw), *pairs))
    images = [image_emb] + [exchange(image_emb, stride) for stride in range(core, near, core)]

    texts[0] = text_emb
    z_names = sorted(z_order, key=lambda j: -j)
    shards = [(texts[0], [(0, 0)])]
    for n, j in enumerate(z_names):
        shards.append((texts[j], [(0, j)]))
        held = [0, j] if n == len(z_names) - 1 else [j]
        joint = jnp.concatenate([texts[i] for i in held]) if len(held) > 1 else texts[j]
        shards += [(exchange(joint, c), [(c, i) for i in held]) for c in range(1, core)]
    owner = jnp.stack([dp_index ^ (near * j + c) for c in range(core) for j in range(far)])
    starts = (owner * rows + mp_index * half).astype(jnp.int32)
    ids = (starts[:, None] + jnp.arange(half, dtype=jnp.int32)[None]).reshape(1, -1)
    scale = jnp.broadcast_to(logit_scale[None], (1, rows))
    col, row = block_stats(
        scale, ids, images, pairs, [shard for shard, _ in shards],
        [[c * far + j for c, j in held] for _, held in shards],
    )

    col_steps = [1] * (core > 1) + [near << k for k in reversed(range(far.bit_length() - 1))]
    row_steps = [core << k for k in reversed(range((near // core).bit_length() - 1))]
    while len(col_steps) > 1:
        ((*col,),) = join([[col[0], exchange(col[1], col_steps.pop(0))]], [2])
    while row_steps:
        ((*row,),) = join([[row[0], exchange(row[1], row_steps.pop(0))]], [2 if row_steps else 1])
    row = [row[0]] + [exchange(row[0], 0, m) for m in range(1, mp)]
    col = [col[0], exchange(col[1], col_steps.pop(0))]
    (col_loss,), (row_loss,) = join([col, row], [0, 0])
    return (row_loss.reshape(-1), col_loss.reshape(-1))


def solution(mesh):
    in_specs = (P("dp", "mp"), P("mp", None), P("dp", "mp"), P("mp", None), P("dp"), P())
    out_specs = (P("dp"), P(("dp", "mp")))
    return jax.shard_map(
        on_device, mesh=mesh, in_specs=in_specs, out_specs=out_specs, check_vma=False
    )
```

```python
import functools

import jax
import jax.numpy as jnp
from jax import lax
from jax.experimental import pallas as pl
from jax.experimental.pallas import tpu as pltpu
from jax.sharding import PartitionSpec as P


def exchange(value, stride, step=0):
    dp, mp = lax.axis_size("dp"), lax.axis_size("mp")
    pairs = [(i * mp + j, (i ^ stride) * mp + (j ^ step)) for i in range(dp) for j in range(mp)]
    return lax.ppermute(value, ("dp", "mp"), pairs)


def normalize(raw):
    norm_sq = jnp.sum(raw * raw, axis=1, keepdims=True)
    return (raw / jnp.sqrt(norm_sq + 1e-06)).astype(jnp.bfloat16)


def stats_kernel(n_image, places, n_col, scale_ref, id_ref, *refs):
    refs = list(refs)
    texts = [refs.pop(0)]
    images = [refs.pop(0) for _ in range(n_image)]
    pairs = [refs.pop(0) for _ in range(n_image)]
    texts += [refs.pop(0) for _ in places[1:]]
    half = texts[0].shape[0]
    blocks = {}
    for held, text in zip(places, texts):
        blocks.update({place: text[n * half : (n + 1) * half, :] for n, place in enumerate(held)})
    texts = [blocks[place] for place in sorted(blocks)]
    col_out, row_out = refs[:n_col], refs[n_col:]
    rows = images[0].shape[0]
    image = jnp.concatenate([r[...] for r in images], axis=0)
    text = jnp.concatenate(texts, axis=0)
    logits = scale_ref[0:1, 0:1] * lax.dot_general(
        image, text, (((1,), (1,)), ((), ())), preferred_element_type=jnp.float32
    )
    ids = id_ref[...]
    pair = jnp.concatenate([jnp.broadcast_to(r[...], (rows, rows)).T for r in pairs], axis=0)
    pair = jnp.concatenate([pair] * (len(texts) * half // rows), axis=1)
    picked = jnp.where(pair == ids, logits, 0.0)

    top = jnp.max(logits, axis=0, keepdims=True)
    lse = top + jnp.log(jnp.sum(jnp.exp(logits - top), axis=0, keepdims=True))
    positive = jnp.sum(picked, axis=0, keepdims=True)
    write(col_out, lse, positive)

    top = jnp.max(logits, axis=1, keepdims=True)
    lse = top + jnp.log(jnp.sum(jnp.exp(logits - top), axis=1, keepdims=True))
    positive = jnp.sum(picked, axis=1, keepdims=True)
    lane = lax.broadcasted_iota(jnp.int32, (image.shape[0], rows), 1)
    both = jnp.where(lane == 0, lse, positive).T
    write(row_out, both[0:1], both[1:2])


def write(outs, lse, positive):
    count = lse.shape[1] // len(outs)
    for k, out in enumerate(outs):
        out[0:1, :] = lse[:, k * count : (k + 1) * count]
        out[1:2, :] = positive[:, k * count : (k + 1) * count]


def pieces(count, n):
    return [jax.ShapeDtypeStruct((2, count // n), jnp.float32)] * n


def block_stats(scale, ids, images, pairs, texts, places):
    rows = images[0].shape[0]
    count = sum(text.shape[0] for text in texts)
    vmem = pl.BlockSpec(memory_space=pltpu.VMEM)
    operands = [scale, ids, texts[0], *images, *pairs, *texts[1:]]
    col = pieces(count, 2)
    row = pieces(rows * len(images), min(2, len(images)))
    out = pl.pallas_call(
        functools.partial(stats_kernel, len(images), places, len(col)),
        out_shape=col + row,
        in_specs=[vmem] * len(operands),
        out_specs=[vmem] * len(col + row),
        compiler_params=pltpu.CompilerParams(vmem_limit_bytes=48 * 2**20),
        cost_estimate=pl.CostEstimate(
            flops=2 * rows * len(images) * count * images[0].shape[1],
            bytes_accessed=sum(o.size * o.dtype.itemsize for o in operands),
            transcendentals=2 * rows * len(images) * count,
        ),
    )(*operands)
    return out[: len(col)], out[len(col) :]


def joined(parts):
    top = functools.reduce(jnp.maximum, [p[0:1, :] for p in parts])
    total = sum(jnp.exp(p[0:1, :] - top) for p in parts)
    return top + jnp.log(total), sum(p[1:2, :] for p in parts)


def join_kernel(counts, splits, *refs):
    refs = list(refs)
    groups = [[refs.pop(0) for _ in range(n)] for n in counts]
    for parts, n in zip(groups, splits):
        lse, positive = joined(parts)
        if n:
            write([refs.pop(0) for _ in range(n)], lse, positive)
        else:
            refs.pop(0)[...] = lse - positive


def join(groups, splits):
    vmem = pl.BlockSpec(memory_space=pltpu.VMEM)
    parts = [part for group in groups for part in group]
    shapes = [
        pieces(g[0].shape[1], n) if n else [jax.ShapeDtypeStruct((1, g[0].shape[1]), jnp.float32)]
        for g, n in zip(groups, splits)
    ]
    flat = [s for shape in shapes for s in shape]
    out = list(pl.pallas_call(
        functools.partial(join_kernel, [len(g) for g in groups], splits),
        out_shape=flat,
        in_specs=[vmem] * len(parts),
        out_specs=[vmem] * len(flat),
        compiler_params=pltpu.CompilerParams(vmem_limit_bytes=4 * 2**20),
    )(*parts))
    return [[out.pop(0) for _ in shape] for shape in shapes]


def on_device(image_feat, image_proj, text_feat, text_proj, pair_index, logit_scale):
    dp = lax.axis_size("dp")
    mp = lax.axis_size("mp")
    dp_index = lax.axis_index("dp")
    mp_index = lax.axis_index("mp")
    far = 1 << ((dp.bit_length() - 1) // 2)
    near = dp // far
    core = min(2, near)
    rows = image_feat.shape[0]
    half = rows // mp
    width = text_proj.shape[1]
    far_order = list(reversed(range(1, far)))

    def text_rows(owner):
        mine = lax.dynamic_slice_in_dim(text_feat, owner * half, half, 0)
        return jnp.dot(mine, text_proj, preferred_element_type=jnp.float32)

    got = [
        exchange(text_rows(mp_index ^ step).astype(jnp.float16), 0, step)
        for step in range(1, mp)
    ]
    image_raw = jnp.dot(image_feat, image_proj, preferred_element_type=jnp.float32)
    sent = image_raw.astype(jnp.float16)
    for step in range(1, mp):
        image_raw = image_raw + exchange(sent, 0, step)
    text_emb = normalize(sum(got, lax.optimization_barrier(text_rows(mp_index))))

    texts = {j: exchange(text_emb, near * j) for j in far_order}

    pairs = [pair_index[None]]
    pairs += [exchange(pairs[0], stride) for stride in range(core, near, core)]
    image_emb, *pairs = lax.optimization_barrier((normalize(image_raw), *pairs))
    images = [image_emb] + [exchange(image_emb, stride) for stride in range(core, near, core)]

    texts[0] = text_emb
    shards = [(texts[0], [(0, 0)])]
    for n, j in enumerate(far_order):
        shards.append((texts[j], [(0, j)]))
        held = [0, j] if n == far - 2 else [j]
        joint = jnp.concatenate([texts[i] for i in held]) if len(held) > 1 else texts[j]
        shards += [(exchange(joint, c), [(c, i) for i in held]) for c in range(1, core)]
    owner = jnp.stack([dp_index ^ (near * j + c) for c in range(core) for j in range(far)])
    starts = (owner * rows + mp_index * half).astype(jnp.int32)
    ids = (starts[:, None] + jnp.arange(half, dtype=jnp.int32)[None]).reshape(1, -1)
    scale = jnp.broadcast_to(logit_scale[None], (1, rows))
    col, row = block_stats(
        scale, ids, images, pairs, [shard for shard, _ in shards],
        [[c * far + j for c, j in held] for _, held in shards],
    )

    col_steps = [1] * (core > 1) + [near << k for k in reversed(range(far.bit_length() - 1))]
    row_steps = [core << k for k in reversed(range((near // core).bit_length() - 1))]
    while len(col_steps) > 1:
        ((*col,),) = join([[col[0], exchange(col[1], col_steps.pop(0))]], [2])
    while row_steps:
        ((*row,),) = join([[row[0], exchange(row[1], row_steps.pop(0))]], [2 if row_steps else 1])
    row = [row[0]] + [exchange(row[0], 0, m) for m in range(1, mp)]
    col = [col[0], exchange(col[1], col_steps.pop(0))]
    (col_loss,), (row_loss,) = join([col, row], [0, 0])
    return (row_loss.reshape(-1), col_loss.reshape(-1))


def solution(mesh):
    in_specs = (P("dp", "mp"), P("mp", None), P("dp", "mp"), P("mp", None), P("dp"), P())
    out_specs = (P("dp"), P(("dp", "mp")))
    return jax.shard_map(
        on_device, mesh=mesh, in_specs=in_specs, out_specs=out_specs, check_vma=False
    )
```

```python
import functools

import jax
import jax.numpy as jnp
from jax import lax
from jax.experimental import pallas as pl
from jax.experimental.pallas import tpu as pltpu
from jax.sharding import PartitionSpec as P


def exchange(value, stride, step=0):
    dp, mp = lax.axis_size("dp"), lax.axis_size("mp")
    pairs = [(i * mp + j, (i ^ stride) * mp + (j ^ step)) for i in range(dp) for j in range(mp)]
    return lax.ppermute(value, ("dp", "mp"), pairs)


def normalize_kernel(raw_ref, out_ref):
    raw = raw_ref[...]
    norm_sq = jnp.sum(raw * raw, axis=1, keepdims=True)
    out_ref[...] = (raw / jnp.sqrt(norm_sq + 1e-06)).astype(jnp.bfloat16)


def normalize(raw):
    vmem = pl.BlockSpec(memory_space=pltpu.VMEM)
    return pl.pallas_call(
        normalize_kernel,
        out_shape=jax.ShapeDtypeStruct(raw.shape, jnp.bfloat16),
        in_specs=[vmem],
        out_specs=vmem,
        compiler_params=pltpu.CompilerParams(vmem_limit_bytes=8 * 2**20),
    )(raw)


def stats_kernel(n_image, places, n_col, scale_ref, id_ref, *refs):
    refs = list(refs)
    texts = [refs.pop(0)]
    images = [refs.pop(0) for _ in range(n_image)]
    pairs = [refs.pop(0) for _ in range(n_image)]
    texts += [refs.pop(0) for _ in places[1:]]
    half = texts[0].shape[0]
    blocks = {}
    for held, text in zip(places, texts):
        blocks.update({place: text[n * half : (n + 1) * half, :] for n, place in enumerate(held)})
    texts = [blocks[place] for place in sorted(blocks)]
    col_out, row_out = refs[:n_col], refs[n_col:]
    rows = images[0].shape[0]
    image = jnp.concatenate([r[...] for r in images], axis=0)
    text = jnp.concatenate(texts, axis=0)
    logits = scale_ref[0:1, 0:1] * lax.dot_general(
        image, text, (((1,), (1,)), ((), ())), preferred_element_type=jnp.float32
    )
    ids = id_ref[...]
    pair = jnp.concatenate([jnp.broadcast_to(r[...], (rows, rows)).T for r in pairs], axis=0)
    pair = jnp.concatenate([pair] * (len(texts) * half // rows), axis=1)
    picked = jnp.where(pair == ids, logits, 0.0)

    top = jnp.max(logits, axis=0, keepdims=True)
    lse = top + jnp.log(jnp.sum(jnp.exp(logits - top), axis=0, keepdims=True))
    positive = jnp.sum(picked, axis=0, keepdims=True)
    write(col_out, lse, positive)

    top = jnp.max(logits, axis=1, keepdims=True)
    lse = top + jnp.log(jnp.sum(jnp.exp(logits - top), axis=1, keepdims=True))
    positive = jnp.sum(picked, axis=1, keepdims=True)
    lane = lax.broadcasted_iota(jnp.int32, (image.shape[0], rows), 1)
    both = jnp.where(lane == 0, lse, positive).T
    write(row_out, both[0:1], both[1:2])


def write(outs, lse, positive):
    count = lse.shape[1] // len(outs)
    for k, out in enumerate(outs):
        out[0:1, :] = lse[:, k * count : (k + 1) * count]
        out[1:2, :] = positive[:, k * count : (k + 1) * count]


def pieces(count, n):
    return [jax.ShapeDtypeStruct((2, count // n), jnp.float32)] * n


def block_stats(scale, ids, images, pairs, texts, places):
    rows = images[0].shape[0]
    count = sum(text.shape[0] for text in texts)
    vmem = pl.BlockSpec(memory_space=pltpu.VMEM)
    operands = [scale, ids, texts[0], *images, *pairs, *texts[1:]]
    col = pieces(count, 2)
    row = pieces(rows * len(images), min(2, len(images)))
    out = pl.pallas_call(
        functools.partial(stats_kernel, len(images), places, len(col)),
        out_shape=col + row,
        in_specs=[vmem] * len(operands),
        out_specs=[vmem] * len(col + row),
        compiler_params=pltpu.CompilerParams(vmem_limit_bytes=48 * 2**20),
        cost_estimate=pl.CostEstimate(
            flops=2 * rows * len(images) * count * images[0].shape[1],
            bytes_accessed=sum(o.size * o.dtype.itemsize for o in operands),
            transcendentals=2 * rows * len(images) * count,
        ),
    )(*operands)
    return out[: len(col)], out[len(col) :]


def joined(parts):
    top = functools.reduce(jnp.maximum, [p[0:1, :] for p in parts])
    total = sum(jnp.exp(p[0:1, :] - top) for p in parts)
    return top + jnp.log(total), sum(p[1:2, :] for p in parts)


def join_kernel(counts, splits, *refs):
    refs = list(refs)
    groups = [[refs.pop(0) for _ in range(n)] for n in counts]
    for parts, n in zip(groups, splits):
        lse, positive = joined(parts)
        if n:
            write([refs.pop(0) for _ in range(n)], lse, positive)
        else:
            refs.pop(0)[...] = lse - positive


def join(groups, splits):
    vmem = pl.BlockSpec(memory_space=pltpu.VMEM)
    parts = [part for group in groups for part in group]
    shapes = [
        pieces(g[0].shape[1], n) if n else [jax.ShapeDtypeStruct((1, g[0].shape[1]), jnp.float32)]
        for g, n in zip(groups, splits)
    ]
    flat = [s for shape in shapes for s in shape]
    out = list(pl.pallas_call(
        functools.partial(join_kernel, [len(g) for g in groups], splits),
        out_shape=flat,
        in_specs=[vmem] * len(parts),
        out_specs=[vmem] * len(flat),
        compiler_params=pltpu.CompilerParams(vmem_limit_bytes=4 * 2**20),
    )(*parts))
    return [[out.pop(0) for _ in shape] for shape in shapes]


def on_device(image_feat, image_proj, text_feat, text_proj, pair_index, logit_scale):
    dp = lax.axis_size("dp")
    mp = lax.axis_size("mp")
    dp_index = lax.axis_index("dp")
    mp_index = lax.axis_index("mp")
    far = 1 << ((dp.bit_length() - 1) // 2)
    near = dp // far
    core = min(2, near)
    rows = image_feat.shape[0]
    half = rows // mp
    width = text_proj.shape[1]
    z_order = list(reversed(range(1, far)))

    def text_rows(owner):
        mine = lax.dynamic_slice_in_dim(text_feat, owner * half, half, 0)
        return jnp.dot(mine, text_proj, preferred_element_type=jnp.float32)

    got = [
        exchange(text_rows(mp_index ^ step).astype(jnp.float16), 0, step)
        for step in range(1, mp)
    ]
    image_raw = jnp.dot(image_feat, image_proj, preferred_element_type=jnp.float32)
    sent = image_raw.astype(jnp.float16)
    for step in range(1, mp):
        image_raw = image_raw + exchange(sent, 0, step)
    text_emb = normalize(sum(got, lax.optimization_barrier(text_rows(mp_index))))

    texts = {j: exchange(text_emb, near * j) for j in z_order}

    pairs = [pair_index[None]]
    pairs += [exchange(pairs[0], stride) for stride in range(core, near, core)]
    image_emb, *pairs = lax.optimization_barrier((normalize(image_raw), *pairs))
    images = [image_emb] + [exchange(image_emb, stride) for stride in range(core, near, core)]

    texts[0] = text_emb
    z_names = sorted(z_order, key=lambda j: -j)
    shards = [(texts[0], [(0, 0)])]
    for n, j in enumerate(z_names):
        shards.append((texts[j], [(0, j)]))
        held = [0, j] if n == len(z_names) - 1 else [j]
        joint = jnp.concatenate([texts[i] for i in held]) if len(held) > 1 else texts[j]
        shards += [(exchange(joint, c), [(c, i) for i in held]) for c in range(1, core)]
    owner = jnp.stack([dp_index ^ (near * j + c) for c in range(core) for j in range(far)])
    starts = (owner * rows + mp_index * half).astype(jnp.int32)
    ids = (starts[:, None] + jnp.arange(half, dtype=jnp.int32)[None]).reshape(1, -1)
    scale = jnp.broadcast_to(logit_scale[None], (1, rows))
    col, row = block_stats(
        scale, ids, images, pairs, [shard for shard, _ in shards],
        [[c * far + j for c, j in held] for _, held in shards],
    )

    col_steps = [1] * (core > 1) + [near << k for k in reversed(range(far.bit_length() - 1))]
    row_steps = [core << k for k in reversed(range((near // core).bit_length() - 1))]
    while len(col_steps) > 1:
        ((*col,),) = join([[col[0], exchange(col[1], col_steps.pop(0))]], [2])
    while row_steps:
        ((*row,),) = join([[row[0], exchange(row[1], row_steps.pop(0))]], [2 if row_steps else 1])
    row = [row[0]] + [exchange(row[0], 0, m) for m in range(1, mp)]
    col = [col[0], exchange(col[1], col_steps.pop(0))]
    (col_loss,), (row_loss,) = join([col, row], [0, 0])
    return (row_loss.reshape(-1), col_loss.reshape(-1))


def solution(mesh):
    in_specs = (P("dp", "mp"), P("mp", None), P("dp", "mp"), P("mp", None), P("dp"), P())
    out_specs = (P("dp"), P(("dp", "mp")))
    return jax.shard_map(
        on_device, mesh=mesh, in_specs=in_specs, out_specs=out_specs, check_vma=False
    )
```

```python
import functools

import jax
import jax.numpy as jnp
from jax import lax
from jax.experimental import pallas as pl
from jax.experimental.pallas import tpu as pltpu
from jax.sharding import PartitionSpec as P


LOG2_E = 1.4426950408889634


def exchange(value, stride, step=0):
    dp, mp = lax.axis_size("dp"), lax.axis_size("mp")
    pairs = [(i * mp + j, (i ^ stride) * mp + (j ^ step)) for i in range(dp) for j in range(mp)]
    return lax.ppermute(value, ("dp", "mp"), pairs)


def normalize_kernel(raw_ref, out_ref):
    raw = raw_ref[...]
    norm_sq = jnp.sum(raw * raw, axis=1, keepdims=True)
    out_ref[...] = (raw / jnp.sqrt(norm_sq + 1e-06)).astype(jnp.bfloat16)


def normalize(raw):
    vmem = pl.BlockSpec(memory_space=pltpu.VMEM)
    return pl.pallas_call(
        normalize_kernel,
        out_shape=jax.ShapeDtypeStruct(raw.shape, jnp.bfloat16),
        in_specs=[vmem],
        out_specs=vmem,
        compiler_params=pltpu.CompilerParams(vmem_limit_bytes=8 * 2**20),
    )(raw)


def stats_kernel(n_image, places, n_col, scale_ref, id_ref, *refs):
    refs = list(refs)
    texts = [refs.pop(0)]
    images = [refs.pop(0) for _ in range(n_image)]
    pairs = [refs.pop(0) for _ in range(n_image)]
    texts += [refs.pop(0) for _ in places[1:]]
    half = texts[0].shape[0]
    blocks = {}
    for held, text in zip(places, texts):
        blocks.update({place: text[n * half : (n + 1) * half, :] for n, place in enumerate(held)})
    texts = [blocks[place] for place in sorted(blocks)]
    col_out, row_out = refs[:n_col], refs[n_col:]
    rows = images[0].shape[0]
    image = jnp.concatenate([r[...] for r in images], axis=0)
    text = jnp.concatenate(texts, axis=0)
    logits = (scale_ref[0:1, 0:1] * LOG2_E) * lax.dot_general(
        image, text, (((1,), (1,)), ((), ())), preferred_element_type=jnp.float32
    )
    ids = id_ref[...]
    pair = jnp.concatenate([jnp.broadcast_to(r[...], (rows, rows)).T for r in pairs], axis=0)
    pair = jnp.concatenate([pair] * (len(texts) * half // rows), axis=1)
    picked = jnp.where(pair == ids, logits, 0.0)

    top = jnp.max(logits, axis=0, keepdims=True)
    lse = (top + jnp.log2(jnp.sum(jnp.exp2(logits - top), axis=0, keepdims=True))) / LOG2_E
    positive = jnp.sum(picked, axis=0, keepdims=True) / LOG2_E
    write(col_out, lse, positive)

    top = jnp.max(logits, axis=1, keepdims=True)
    lse = (top + jnp.log2(jnp.sum(jnp.exp2(logits - top), axis=1, keepdims=True))) / LOG2_E
    positive = jnp.sum(picked, axis=1, keepdims=True) / LOG2_E
    lane = lax.broadcasted_iota(jnp.int32, (image.shape[0], rows), 1)
    both = jnp.where(lane == 0, lse, positive).T
    write(row_out, both[0:1], both[1:2])


def write(outs, lse, positive):
    count = lse.shape[1] // len(outs)
    for k, out in enumerate(outs):
        out[0:1, :] = lse[:, k * count : (k + 1) * count]
        out[1:2, :] = positive[:, k * count : (k + 1) * count]


def pieces(count, n):
    return [jax.ShapeDtypeStruct((2, count // n), jnp.float32)] * n


def block_stats(scale, ids, images, pairs, texts, places):
    rows = images[0].shape[0]
    count = sum(text.shape[0] for text in texts)
    vmem = pl.BlockSpec(memory_space=pltpu.VMEM)
    operands = [scale, ids, texts[0], *images, *pairs, *texts[1:]]
    col = pieces(count, 2)
    row = pieces(rows * len(images), min(2, len(images)))
    out = pl.pallas_call(
        functools.partial(stats_kernel, len(images), places, len(col)),
        out_shape=col + row,
        in_specs=[vmem] * len(operands),
        out_specs=[vmem] * len(col + row),
        compiler_params=pltpu.CompilerParams(vmem_limit_bytes=48 * 2**20),
        cost_estimate=pl.CostEstimate(
            flops=2 * rows * len(images) * count * images[0].shape[1],
            bytes_accessed=sum(o.size * o.dtype.itemsize for o in operands),
            transcendentals=2 * rows * len(images) * count,
        ),
    )(*operands)
    return out[: len(col)], out[len(col) :]


def joined(parts):
    top = functools.reduce(jnp.maximum, [p[0:1, :] for p in parts])
    total = sum(jnp.exp(p[0:1, :] - top) for p in parts)
    return top + jnp.log(total), sum(p[1:2, :] for p in parts)


def join_kernel(counts, splits, *refs):
    refs = list(refs)
    groups = [[refs.pop(0) for _ in range(n)] for n in counts]
    for parts, n in zip(groups, splits):
        lse, positive = joined(parts)
        if n:
            write([refs.pop(0) for _ in range(n)], lse, positive)
        else:
            refs.pop(0)[...] = lse - positive


def join(groups, splits):
    vmem = pl.BlockSpec(memory_space=pltpu.VMEM)
    parts = [part for group in groups for part in group]
    shapes = [
        pieces(g[0].shape[1], n) if n else [jax.ShapeDtypeStruct((1, g[0].shape[1]), jnp.float32)]
        for g, n in zip(groups, splits)
    ]
    flat = [s for shape in shapes for s in shape]
    out = list(pl.pallas_call(
        functools.partial(join_kernel, [len(g) for g in groups], splits),
        out_shape=flat,
        in_specs=[vmem] * len(parts),
        out_specs=[vmem] * len(flat),
        compiler_params=pltpu.CompilerParams(vmem_limit_bytes=4 * 2**20),
    )(*parts))
    return [[out.pop(0) for _ in shape] for shape in shapes]


def on_device(image_feat, image_proj, text_feat, text_proj, pair_index, logit_scale):
    dp = lax.axis_size("dp")
    mp = lax.axis_size("mp")
    dp_index = lax.axis_index("dp")
    mp_index = lax.axis_index("mp")
    far = 1 << ((dp.bit_length() - 1) // 2)
    near = dp // far
    core = min(2, near)
    rows = image_feat.shape[0]
    half = rows // mp
    width = text_proj.shape[1]
    z_order = list(reversed(range(1, far)))

    def text_rows(owner):
        mine = lax.dynamic_slice_in_dim(text_feat, owner * half, half, 0)
        return jnp.dot(mine, text_proj, preferred_element_type=jnp.float32)

    got = [
        exchange(text_rows(mp_index ^ step).astype(jnp.float16), 0, step)
        for step in range(1, mp)
    ]
    image_raw = jnp.dot(image_feat, image_proj, preferred_element_type=jnp.float32)
    sent = image_raw.astype(jnp.float16)
    for step in range(1, mp):
        image_raw = image_raw + exchange(sent, 0, step)
    text_emb = normalize(sum(got, lax.optimization_barrier(text_rows(mp_index))))

    texts = {j: exchange(text_emb, near * j) for j in z_order}

    pairs = [pair_index[None]]
    pairs += [exchange(pairs[0], stride) for stride in range(core, near, core)]
    image_emb, *pairs = lax.optimization_barrier((normalize(image_raw), *pairs))
    images = [image_emb] + [exchange(image_emb, stride) for stride in range(core, near, core)]

    texts[0] = text_emb
    z_names = sorted(z_order, key=lambda j: -j)
    shards = [(texts[0], [(0, 0)])]
    for n, j in enumerate(z_names):
        shards.append((texts[j], [(0, j)]))
        held = [0, j] if n == len(z_names) - 1 else [j]
        joint = jnp.concatenate([texts[i] for i in held]) if len(held) > 1 else texts[j]
        shards += [(exchange(joint, c), [(c, i) for i in held]) for c in range(1, core)]
    owner = jnp.stack([dp_index ^ (near * j + c) for c in range(core) for j in range(far)])
    starts = (owner * rows + mp_index * half).astype(jnp.int32)
    ids = (starts[:, None] + jnp.arange(half, dtype=jnp.int32)[None]).reshape(1, -1)
    scale = jnp.broadcast_to(logit_scale[None], (1, rows))
    col, row = block_stats(
        scale, ids, images, pairs, [shard for shard, _ in shards],
        [[c * far + j for c, j in held] for _, held in shards],
    )

    col_steps = [1] * (core > 1) + [near << k for k in reversed(range(far.bit_length() - 1))]
    row_steps = [core << k for k in reversed(range((near // core).bit_length() - 1))]
    while len(col_steps) > 1:
        ((*col,),) = join([[col[0], exchange(col[1], col_steps.pop(0))]], [2])
    while row_steps:
        ((*row,),) = join([[row[0], exchange(row[1], row_steps.pop(0))]], [2 if row_steps else 1])
    row = [row[0]] + [exchange(row[0], 0, m) for m in range(1, mp)]
    col = [col[0], exchange(col[1], col_steps.pop(0))]
    (col_loss,), (row_loss,) = join([col, row], [0, 0])
    return (row_loss.reshape(-1), col_loss.reshape(-1))


def solution(mesh):
    in_specs = (P("dp", "mp"), P("mp", None), P("dp", "mp"), P("mp", None), P("dp"), P())
    out_specs = (P("dp"), P(("dp", "mp")))
    return jax.shard_map(
        on_device, mesh=mesh, in_specs=in_specs, out_specs=out_specs, check_vma=False
    )
```
